32 devices in a mesh: gx: 4 (over x, core), gy: 8 (over z, y).
Axes of the slice: x: 2, y: 2, z: 4, core: 2. Of those that a mesh axis runs over, the one named last changes fastest.
Arguments:
- features: bfloat16 [32, 64, 96, 128], P('gx', 'gy'), may hold values from -6 to 6
- active_mask: int32 [32, 64, 128], P('gx', 'gy'), may hold values 0 or 1
- owners: int32 [4, 8, 16], P('gx', 'gy'), may hold values from 0 to 7, as said below
- weight: bfloat16 [3, 3, 96, 288], replicated, may hold values from -0.125 to 0.125
- channel_bias: float32 [96], replicated, may hold values from -3 to 3
- cotangent: bfloat16 [4, 256, 96, 512], P('gx', 'gy'), may hold values from -6 to 6
Outputs:
- activations: bfloat16 [4, 256, 96, 512], P('gx', 'gy')
- grad_features: bfloat16 [32, 64, 96, 128], P('gx', 'gy')
- grad_weight: float32 [3, 3, 96, 288], replicated
The draws below stay inside these ranges and needn't reach their ends.
Inputs may be any that keep to these rules, and one draw needn't show every extreme that they name: `owners`: of the bricks of one tile at most 4 have the same owner, and in every gx row one owner receives exactly 4 bricks from every tile of the row.
All inputs are finite; a program needn't handle non-finite values. No bound on the sum of `active_mask` on one device may be relied on, other than what follows from the above.
Results may differ from the reference program's by a relative error of at most 0.005.
Values may be sent and summed in bfloat16 or wider, within the bound.
No kernel may reach another device: no remote copies, remote signals or barrier semaphores. Data moves between devices by JAX's collectives and lax.ppermute only.
A program may use at most 320 MiB of HBM per device.

```python
import jax
import jax.numpy as jnp
from jax import lax

C = 96
BY_DEV = 1
BZ = 16
CAP = 4
SLOTS = 32
NX = 32
NY = 64
NZ = 128
NVOX = 262144
N_GX = 4
N_GY = 8


def draw_owners(key, part):
    bricks_dev = BY_DEV * BZ
    devices = N_GX * N_GY
    key_hot, key_pick, key_order = jax.random.split(key, 3)
    hottest = jax.random.randint(key_hot, (N_GX, 1), 0, N_GY)
    labels = jnp.repeat(jnp.arange(1, N_GY, dtype=jnp.int32), CAP)
    chosen = jax.vmap(lambda subkey: jax.random.permutation(subkey, labels)[:bricks_dev - CAP])(jax.random.split(key_pick, devices))
    offsets = jnp.concatenate([jnp.zeros((devices, CAP), jnp.int32), chosen.astype(jnp.int32)], axis=1)
    offsets = jax.vmap(lambda subkey, listing: jax.random.permutation(subkey, listing))(jax.random.split(key_order, devices), offsets)
    owner_ids = (offsets.reshape(N_GX, N_GY * bricks_dev) + hottest) % N_GY
    return owner_ids.reshape(N_GX, N_GY * BY_DEV, BZ).astype(jnp.int32)


def place_ends(drawn, own_key, low, largest):
    dims = drawn.shape
    index_at = [jax.random.randint(jax.random.fold_in(own_key, axis), (), 0, dims[axis]) for axis in range(len(dims))]
    drawn = drawn.at[tuple(index_at)].set(low)
    longest = dims.index(max(dims))
    index_at[longest] = (index_at[longest] + 1) % dims[longest]
    return drawn.at[tuple(index_at)].set(largest)


def shard_levels(stream_key, dims, shards, low, largest):
    def one(dim, blocks):
        draws = jax.random.uniform(jax.random.fold_in(jax.random.fold_in(stream_key, 6), dim), (blocks,), jnp.float32, low / len(shards), largest / len(shards))
        return jnp.repeat(jnp.exp(draws), dims[dim] // blocks).reshape((-1,) + (1,) * (len(dims) - dim - 1))

    gain = one(*shards[0])
    for cut in shards[1:]:
        gain = gain * one(*cut)
    return gain


def scatter_about(stream_key, dims, scale, limit, cuts=(), kind=jnp.bfloat16):
    values = scale * jax.random.normal(stream_key, dims, jnp.float32)
    if cuts:
        values = values * shard_levels(stream_key, dims, cuts, -0.22, 0.18)
    return jnp.clip(values, -limit, limit).astype(kind)


def setup_inputs(seed: int = 0) -> dict:
    key_list = jax.random.split(jax.random.key(seed), 7)
    features = scatter_about(key_list[0], (NX, NY, C, NZ), 1.0, 6.0, ((0, 4), (1, 8)))
    active_mask = place_ends((jax.random.randint(key_list[1], (NX, NY, NZ), 0, 2) < 1).astype(jnp.int32), jax.random.fold_in(key_list[1], 1), 0, 1)
    owners = draw_owners(jax.random.fold_in(key_list[6], 71), 0)
    weight = scatter_about(key_list[3], (3, 3, C, 3 * C), (27 * C) ** -0.5, 0.125)
    channel_bias = scatter_about(key_list[4], (C,), 0.5, 3.0, (), jnp.float32)
    cotangent = scatter_about(key_list[5], (N_GX, N_GY * SLOTS, C, 512), 1.0, 6.0, ((0, 4), (1, 8)))
    return dict(features=features, active_mask=active_mask, owners=owners, weight=weight, channel_bias=channel_bias, cotangent=cotangent)


FORWARD_SPEC = ("NXYCZ", "XYOZI", "NXYCZ")
BACKWARD_SPEC = ("NXYCZ", "XYIZO", "NXYCZ")


def correlate(volume, kernel, spec):
    result = lax.conv_general_dilated(volume[None].astype(jnp.float32), kernel.astype(jnp.float32), (1, 1, 1), ((1, 1), (1, 1), (1, 1)), dimension_numbers=spec, precision=lax.Precision.HIGHEST)
    return result[0]


def slot_of(owners):
    owner_list = owners.reshape(N_GX, N_GY, BY_DEV * BZ)
    matches = (owner_list[..., None] == jnp.arange(N_GY, dtype=jnp.int32)).astype(jnp.int32)
    before = jnp.cumsum(matches, axis=2) - matches
    ranking = jnp.sum(before * matches, axis=3)
    source = jnp.arange(N_GY, dtype=jnp.int32)[None, :, None]
    return owner_list, (source * CAP + ranking).astype(jnp.int32)


def to_bricks(volume):
    channels = volume.shape[2]
    reshaped = volume.reshape(N_GX, 8, N_GY, BY_DEV, 8, channels, BZ, 8)
    reshaped = jnp.transpose(reshaped, (0, 2, 3, 6, 5, 1, 4, 7))
    return reshaped.reshape(N_GX, N_GY, BY_DEV * BZ, channels, 512)


def from_bricks(bricks):
    channels = bricks.shape[3]
    reshaped = bricks.reshape(N_GX, N_GY, BY_DEV, BZ, channels, 8, 8, 8)
    reshaped = jnp.transpose(reshaped, (0, 5, 1, 2, 6, 4, 3, 7))
    return reshaped.reshape(NX, NY, channels, NZ)


def reference(features, active_mask, owners, weight, channel_bias, cotangent):
    active = active_mask.astype(jnp.float32)[:, :, None, :]
    masked_input = features * active_mask.astype(features.dtype)[:, :, None, :]
    kernel = weight.reshape(3, 3, C, 3, C)
    preact = correlate(masked_input, kernel, FORWARD_SPEC) + channel_bias[None, None, :, None]
    gating = jax.nn.sigmoid(preact)
    activated_scene = (active * preact * gating).astype(jnp.bfloat16)
    owner_list, position = slot_of(owners)
    row_index = jnp.arange(N_GX, dtype=jnp.int32)[:, None, None]
    owner_slots = jnp.zeros((N_GX, N_GY, SLOTS, C, 512), jnp.bfloat16)
    owner_slots = owner_slots.at[row_index, owner_list, position].set(to_bricks(activated_scene))
    activations = owner_slots.reshape(N_GX, N_GY * SLOTS, C, 512)
    cotan_bricks = cotangent.reshape(N_GX, N_GY, SLOTS, C, 512)[row_index, owner_list, position]
    cotangent_scene = from_bricks(cotan_bricks)
    slope = (cotangent_scene.astype(jnp.float32) * active * gating * (1.0 + preact * (1.0 - gating))).astype(jnp.bfloat16)
    mirror = kernel[::-1, ::-1, :, ::-1, :]
    grad_features = (active * correlate(slope, mirror, BACKWARD_SPEC)).astype(jnp.bfloat16)
    flat_slope = jnp.transpose(slope, (2, 0, 1, 3)).reshape(C, NX * NY * NZ).astype(jnp.float32)
    spread = jnp.pad(jnp.transpose(masked_input, (2, 0, 1, 3)).astype(jnp.float32), ((0, 0), (1, 1), (1, 1), (1, 1)))

    def one_tap(offset):
        corner = (jnp.int32(0), (offset // 9).astype(jnp.int32), (offset // 3 % 3).astype(jnp.int32), (offset % 3).astype(jnp.int32))
        window = lax.dynamic_slice(spread, corner, (C, NX, NY, NZ)).reshape(C, NX * NY * NZ)
        return jnp.dot(flat_slope, window.T, precision=lax.Precision.HIGHEST)

    tap_sums = lax.map(one_tap, jnp.arange(27, dtype=jnp.int32))
    grad_weight = jnp.transpose(tap_sums.reshape(3, 3, 3, C, C), (0, 1, 3, 2, 4)).reshape(3, 3, C, 3 * C) * (NVOX ** -0.5)
    return activations, grad_features, grad_weight.astype(jnp.float32)
```

```python
import functools

import jax
import jax.numpy as jnp
from jax import lax
from jax.experimental import pallas as pl
from jax.experimental.pallas import tpu as pltpu
from jax.sharding import PartitionSpec as P

BRICK = 8
LANES = 128
GROUP = LANES // BRICK
CHUNK = 32
VMEM_LIMIT = 48 * 2**20


def shift_lanes(value, by):
    width = value.shape[-1]
    lane = lax.broadcasted_iota(jnp.int32, value.shape, value.ndim - 1)
    rolled = pltpu.roll(value, by % width, value.ndim - 1)
    inside = lane >= by if by > 0 else lane < width + by
    return jnp.where(inside, rolled, jnp.zeros_like(rolled))


def swap_blocks(tiles):
    axis = tiles[0].ndim - 1
    block = lax.broadcasted_iota(jnp.int32, tiles[0].shape, axis) // BRICK
    turned = []
    for k in range(GROUP):
        source = -k % GROUP
        tile = tiles[source]
        turned.append(pltpu.roll(tile, BRICK * source, axis) if source else tile)
    step = 1
    while step < GROUP:
        moved = (block // step) % 2 == 1
        turned = [
            jnp.where(moved, turned[(k - step) % GROUP], turned[k]) for k in range(GROUP)
        ]
        step *= 2
    return [
        pltpu.roll(turned[k], LANES - BRICK * k, axis) if k else turned[k] for k in range(GROUP)
    ]


def fill_slots(me_ref, owners_ref, slots_ref, counts_ref, capacity):
    def clear(member, carry):
        counts_ref[member] = 0
        return carry

    lax.fori_loop(0, counts_ref.shape[0], clear, 0)

    def place(brick, carry):
        owner = owners_ref[brick]
        rank = counts_ref[owner]
        slots_ref[brick] = (owner ^ me_ref[0]) * capacity + rank
        counts_ref[owner] = rank + 1
        return carry

    lax.fori_loop(0, slots_ref.shape[0], place, 0)


def copy_all(pairs, sems):
    copies = [
        pltpu.make_async_copy(source, target, sems.at[i])
        for i, (source, target) in enumerate(pairs)
    ]
    for copy in copies:
        copy.start()
    return copies


def columns_of(ref, row, across):
    return jnp.concatenate(
        [ref[row + dx, across + dy] for dx in range(3) for dy in range(3)], axis=0
    )


def conv_two(kernel, ref, row, across):
    channels = ref.shape[2]
    stacked = jnp.concatenate(
        [columns_of(ref, row, across), columns_of(ref, row, across + 1)], axis=1
    )
    product = jnp.dot(kernel, stacked, preferred_element_type=jnp.float32)
    results = []
    for half in range(2):
        part = product[:, half * LANES : (half + 1) * LANES]
        results.append(
            shift_lanes(part[:channels], 1)
            + part[channels : 2 * channels]
            + shift_lanes(part[2 * channels :], -1)
        )
    return results


def fill_padded(padded_ref, y_low, y_high, x_low, x_high):
    rows, across = padded_ref.shape[0] - 2, padded_ref.shape[1] - 2
    for y in range(across + 2):
        padded_ref[0, y] = x_low[0, y]
        padded_ref[rows + 1, y] = x_high[0, y]
    for x in range(rows):
        padded_ref[x + 1, 0] = y_low[x, 0]
        padded_ref[x + 1, across + 1] = y_high[x, 0]


def forward_body(
    members,
    me_ref,
    owners_ref,
    features_ref,
    mask_ref,
    y_low,
    y_high,
    x_low,
    x_high,
    weight_ref,
    bias_ref,
    *refs,
):
    messages, refs = refs[:members], refs[members:]
    padded_ref, factor_ref, backward_ref = refs[:3]
    outgoing_ref, scene_ref, kernel_ref, slots_ref, counts_ref, sems = refs[3:]
    rows, across, channels, _ = features_ref.shape
    capacity = messages[0].shape[0]
    fill_slots(me_ref, owners_ref, slots_ref, counts_ref, capacity)
    fill_padded(padded_ref, y_low, y_high, x_low, x_high)
    for shift in range(3):
        mirrored = slice((2 - shift) * channels, (3 - shift) * channels)
        taken = slice(shift * channels, (shift + 1) * channels)
        for tap in range(9):
            placed = slice(tap * channels, (tap + 1) * channels)
            kernel_ref[taken, placed] = weight_ref[tap, :, taken]
            backward_ref[taken, placed] = weight_ref[8 - tap, :, mirrored].T

    @pl.loop(0, rows)
    def _(x):
        for y in range(across):
            half = mask_ref[x, y : y + 1, :].astype(jnp.float32)
            padded_ref[x + 1, y + 1] = (
                features_ref[x, y].astype(jnp.float32) * half
            ).astype(jnp.bfloat16)

    @pl.loop(0, outgoing_ref.shape[0])
    def _(slot):
        outgoing_ref[slot] = jnp.zeros(outgoing_ref.shape[1:], outgoing_ref.dtype)

    bias = bias_ref[...]

    @pl.loop(0, rows)
    def _(x):
        for y in range(0, across, 2):
            for half, summed in enumerate(conv_two(kernel_ref[...], padded_ref, x, y)):
                preact = summed + bias
                gating = jax.nn.sigmoid(preact)
                active = mask_ref[x, y + half : y + half + 1, :].astype(jnp.float32)
                gated = active * gating
                scene_ref[x * across + y + half] = (preact * gated).astype(scene_ref.dtype)
                factor_ref[x, y + half] = gated * (1.0 + preact * (1.0 - gating))

    for group in range(rows * across // GROUP):

        @pl.loop(0, channels // CHUNK)
        def _(part):
            span = pl.ds(pl.multiple_of(part * CHUNK, CHUNK), CHUNK)
            tiles = swap_blocks([scene_ref[group * GROUP + q, span, :] for q in range(GROUP)])
            for brick in range(GROUP):
                outgoing_ref[
                    slots_ref[brick], span, group * LANES : (group + 1) * LANES
                ] = tiles[brick]

    for copy in copy_all(
        [
            (outgoing_ref.at[k * capacity : (k + 1) * capacity], messages[k])
            for k in range(members)
        ],
        sems,
    ):
        copy.wait()


def slope_body(
    capacity, zero_ref, owners_ref, returned_ref, factor_ref, slope_ref, slots_ref, counts_ref
):
    rows, across, channels, _ = factor_ref.shape
    fill_slots(zero_ref, owners_ref, slots_ref, counts_ref, capacity)
    for group in range(rows * across // GROUP):

        @pl.loop(0, channels // CHUNK)
        def _(part):
            span = pl.ds(pl.multiple_of(part * CHUNK, CHUNK), CHUNK)
            tiles = swap_blocks(
                [
                    returned_ref[
                        slots_ref[brick], span, group * LANES : (group + 1) * LANES
                    ]
                    for brick in range(GROUP)
                ]
            )
            for q in range(GROUP):
                x, y = (group * GROUP + q) // across, (group * GROUP + q) % across
                slope_ref[x, y, span, :] = (
                    tiles[q].astype(jnp.float32) * factor_ref[x, y, span, :]
                ).astype(slope_ref.dtype)


def kernel_grad_body(slope_ref, padded_ref, parts_ref, total_ref):
    rows, across, channels, _ = slope_ref.shape
    total_ref[...] = jnp.zeros_like(total_ref)

    @pl.loop(0, rows)
    def _(x):
        for y in range(0, across, 2):
            shifted = []
            for half in range(2):
                block = slope_ref[x, y + half].astype(jnp.float32)
                shifted.append(
                    jnp.concatenate(
                        [shift_lanes(block, -1), block, shift_lanes(block, 1)], axis=0
                    ).astype(jnp.bfloat16)
                )
            left = jnp.concatenate(shifted, axis=1)
            right = jnp.concatenate(
                [columns_of(padded_ref, x, y), columns_of(padded_ref, x, y + 1)], axis=1
            )
            total_ref[...] += lax.dot_general(
                left, right, (((1,), (1,)), ((), ())), preferred_element_type=jnp.float32
            )

    split, _, share, _ = parts_ref.shape
    for part in range(split):
        for shift in range(3):
            start = shift * channels + part * share
            parts_ref[part, shift] = total_ref[start : start + share, :]


def finish_body(scale, at_ref, *refs):
    pieces, out_ref, shares_ref = refs[:-2], refs[-2], refs[-1]
    split, _, share, _ = shares_ref.shape
    for index, piece in enumerate(pieces):
        shares_ref[at_ref[index]] = piece[...].astype(jnp.float32) * scale
    channels = split * share
    for part in range(split):
        for shift in range(3):
            for tap in range(9):
                out_ref[
                    tap,
                    part * share : (part + 1) * share,
                    shift * channels : (shift + 1) * channels,
                ] = shares_ref[part, shift, :, tap * channels : (tap + 1) * channels]


def features_grad_body(
    slope_ref,
    mask_ref,
    y_low,
    y_high,
    x_low,
    x_high,
    kernel_ref,
    out_ref,
    padded_ref,
):
    rows, across, channels, _ = slope_ref.shape
    fill_padded(padded_ref, y_low, y_high, x_low, x_high)

    @pl.loop(0, rows)
    def _(x):
        for y in range(across):
            padded_ref[x + 1, y + 1] = slope_ref[x, y]

    @pl.loop(0, rows)
    def _(x):
        for y in range(0, across, 2):
            for half, summed in enumerate(conv_two(kernel_ref[...], padded_ref, x, y)):
                active = mask_ref[x, y + half : y + half + 1, :].astype(jnp.float32)
                out_ref[x, y + half] = (active * summed).astype(out_ref.dtype)


def call(body, outs, specs, out_specs, scratch, args, flops, bytes_accessed, transcendentals=0):
    return pl.pallas_call(
        body,
        out_shape=outs,
        in_specs=specs,
        out_specs=out_specs,
        scratch_shapes=scratch,
        compiler_params=pltpu.CompilerParams(vmem_limit_bytes=VMEM_LIMIT),
        cost_estimate=pl.CostEstimate(
            flops=flops, bytes_accessed=bytes_accessed, transcendentals=transcendentals
        ),
    )(*args)


def after(values, *others):
    return lax.optimization_barrier((tuple(values), others))[0]


def from_neighbours(low_edge, high_edge, axis):
    count = lax.axis_size(axis)
    forward = [(i, i + 1) for i in range(count - 1)]
    backward = [(target, source) for source, target in forward]
    return lax.ppermute(high_edge, axis, forward), lax.ppermute(low_edge, axis, backward)


def halo_rows(rows, y_low, y_high):
    pieces = (slice(0, 1), slice(-1, None))
    return from_neighbours(
        *[
            jnp.concatenate([y_low[piece], row, y_high[piece]], axis=1)
            for row, piece in zip(rows, pieces)
        ],
        "gx",
    )


def edge_of(array):
    def edge(side, along_x):
        piece = slice(0, 1) if side == 0 else slice(-1, None)
        return array[piece] if along_x else array[:, piece]

    return edge


def from_group(value, axis, radix, stride):
    count = lax.axis_size(axis)
    return [
        lax.ppermute(value, axis, [(i, i ^ (k * stride)) for i in range(count)])
        for k in range(1, radix)
    ]


def to_members(blocks, differences):
    count = lax.axis_size("gy")
    return {
        k: lax.ppermute(blocks[k], "gy", [(i, i ^ k) for i in range(count)]) for k in differences
    }


def on_device(features, active_mask, owners, weight, channel_bias, cotangent):
    rows, across, channels, column = features.shape
    members_x, members = lax.axis_size("gx"), lax.axis_size("gy")
    at_x, me = lax.axis_index("gx"), lax.axis_index("gy")
    capacity = cotangent.shape[1] // members
    slot_count = members * capacity
    brick = cotangent.shape[3]
    vmem = pl.BlockSpec(memory_space=pltpu.VMEM)
    smem = pl.BlockSpec(memory_space=pltpu.SMEM)
    anywhere = pl.BlockSpec(memory_space=pltpu.HBM)
    conv_flops = 2 * rows * across * column * 27 * channels * channels
    scene_bytes = rows * across * column * channels
    far = [list(range(members // 2, members))[i::4] for i in range(4)]
    near = list(range(1, members // 2))
    message = (capacity, channels, brick)
    packed = jax.ShapeDtypeStruct(message, jnp.bfloat16)

    def masked(scene):
        def edge(side, along_x):
            mask = edge_of(active_mask)(side, along_x).astype(jnp.bfloat16)
            return edge_of(scene)(side, along_x) * mask[:, :, None, :]

        return edge

    columns = [masked(features)(side, False) for side in (0, -1)]
    halo = from_neighbours(*columns, "gy")
    rows_beside = [masked(features)(side, True) for side in (0, -1)]
    (owned,) = after([cotangent], *halo)
    returned = lax.all_to_all(
        owned.reshape(members, capacity * channels, brick),
        "gy",
        split_axis=0,
        concat_axis=0,
        tiled=True,
    ).reshape(slot_count, channels, brick)
    halo = (*halo, *halo_rows(rows_beside, *halo))

    me_list = me.reshape(1).astype(jnp.int32)
    owner_list = owners.reshape(-1)
    table = [pltpu.SMEM((owner_list.size,), jnp.int32), pltpu.SMEM((members,), jnp.int32)]
    slots = pltpu.VMEM((slot_count, channels, brick), jnp.bfloat16)
    sems = pltpu.SemaphoreType.DMA((members,))
    padded_shape = (rows + 2, across + 2, channels, column)
    kernel_shape = (3 * channels, 9 * channels)
    *outgoing, padded, factor, backward_kernel = call(
        functools.partial(forward_body, members),
        (
            *[packed] * members,
            jax.ShapeDtypeStruct(padded_shape, jnp.bfloat16),
            jax.ShapeDtypeStruct(features.shape, jnp.float32),
            jax.ShapeDtypeStruct(kernel_shape, jnp.bfloat16),
        ),
        [smem] * 2 + [vmem] * 8,
        [anywhere] * members + [vmem] * 3,
        [
            slots,
            pltpu.VMEM((rows * across, channels, column), jnp.bfloat16),
            pltpu.VMEM(kernel_shape, jnp.bfloat16),
            *table,
            sems,
        ],
        (
            me_list,
            owner_list,
            features,
            active_mask,
            *halo,
            weight.reshape(9, channels, 3 * channels),
            channel_bias.reshape(channels, 1),
        ),
        conv_flops,
        14 * scene_bytes,
        2 * scene_bytes,
    )
    arrived = {0: outgoing[0]}

    def send(differences, *others):
        messages = after([outgoing[k] for k in differences], *others)
        arrived.update(to_members(dict(zip(differences, messages)), differences))

    arrived.update(to_members(outgoing, near))
    (returned,) = after([returned], *[arrived[k] for k in near])
    slope = call(
        functools.partial(slope_body, capacity),
        jax.ShapeDtypeStruct(features.shape, jnp.bfloat16),
        [smem] * 2 + [vmem] * 2,
        vmem,
        [*table],
        (jnp.zeros((1,), jnp.int32), owner_list, returned, factor),
        0,
        0,
    )

    def in_turn(value, index):
        return after([value], *[arrived[k] for k in far[index]])[0]

    send(far[0], returned)
    send(far[1], returned)
    shares = call(
        kernel_grad_body,
        jax.ShapeDtypeStruct((members_x, 3, channels // members_x, 9 * channels), jnp.float32),
        [vmem] * 2,
        vmem,
        [pltpu.VMEM(kernel_shape, jnp.float32)],
        (slope, padded),
        0,
        0,
    )
    send(far[2], shares)
    shares = in_turn(shares, 0)
    total = lax.dynamic_index_in_dim(shares, at_x, 0, keepdims=False)
    for k in range(1, members_x):
        wanted = lax.dynamic_index_in_dim(shares, at_x ^ k, 0, keepdims=False)
        total = total + lax.ppermute(
            wanted.astype(jnp.bfloat16), "gx", [(i, i ^ k) for i in range(members_x)]
        ).astype(jnp.float32)
    columns = [edge_of(slope)(side, False) for side in (0, -1)]
    slope_halo = from_neighbours(*after(columns, total), "gy")
    for index, (radix, stride) in enumerate(((members // 4, 1), (4, members // 4))):
        total = in_turn(total, index + 1)
        sent = total.astype(jnp.bfloat16)
        terms = [
            term.astype(jnp.float32) for term in [sent, *from_group(sent, "gy", radix, stride)]
        ]
        while len(terms) > 1:
            terms = [terms[i] + terms[i + 1] for i in range(0, len(terms), 2)]
        total = terms[0]
        if index == 0:
            send(far[3], total)
    mine = total.astype(jnp.bfloat16)
    at_shares = jnp.stack([at_x ^ k for k in range(members_x)]).astype(jnp.int32)
    pieces = [mine, *from_group(mine, "gx", members_x, 1)]
    pieces = after(pieces, *[arrived[k] for k in far[3]])
    voxel_total = rows * across * column * members_x * members
    grad_weight = call(
        functools.partial(finish_body, voxel_total ** (-0.5)),
        jax.ShapeDtypeStruct((9, channels, 3 * channels), jnp.float32),
        [smem] + [vmem] * members_x,
        vmem,
        [pltpu.VMEM(shares.shape, jnp.float32)],
        (at_shares, *pieces),
        weight.size,
        6 * weight.size,
    ).reshape(weight.shape)
    rows_beside = [edge_of(slope)(side, True) for side in (0, -1)]
    slope_halo = (*slope_halo, *halo_rows(rows_beside, *slope_halo))
    grad_features = call(
        features_grad_body,
        jax.ShapeDtypeStruct(features.shape, jnp.bfloat16),
        [vmem] * 7,
        vmem,
        [pltpu.VMEM(padded_shape, jnp.bfloat16)],
        (slope, active_mask, *slope_halo, backward_kernel),
        conv_flops,
        5 * scene_bytes,
    )
    activations = jnp.zeros((members, *message), jnp.bfloat16)
    for k in [0, *near, *far[0], *far[1], *far[2], *far[3]]:
        activations = lax.dynamic_update_index_in_dim(activations, arrived[k], me ^ k, 0)
    activations = activations.reshape(1, slot_count, channels, brick)
    return activations, grad_features, grad_weight


def solution(mesh):
    in_specs = (
        P("gx", "gy", None, None),
        P("gx", "gy", None),
        P("gx", "gy", None),
        P(),
        P(),
        P("gx", "gy", None, None),
    )
    out_specs = (P("gx", "gy", None, None), P("gx", "gy", None, None), P())
    return jax.shard_map(
        on_device, mesh=mesh, in_specs=in_specs, out_specs=out_specs, check_vma=False
    )
```

```python
import functools

import jax
import jax.numpy as jnp
from jax import lax
from jax.experimental import pallas as pl
from jax.experimental.pallas import tpu as pltpu
from jax.sharding import PartitionSpec as P

BRICK = 8
LANES = 128
GROUP = LANES // BRICK
CHUNK = 32
VMEM_LIMIT = 48 * 2**20


def shift_lanes(value, by):
    width = value.shape[-1]
    lane = lax.broadcasted_iota(jnp.int32, value.shape, value.ndim - 1)
    rolled = pltpu.roll(value, by % width, value.ndim - 1)
    inside = lane >= by if by > 0 else lane < width + by
    return jnp.where(inside, rolled, jnp.zeros_like(rolled))


def swap_blocks(tiles):
    axis = tiles[0].ndim - 1
    block = lax.broadcasted_iota(jnp.int32, tiles[0].shape, axis) // BRICK
    turned = []
    for k in range(GROUP):
        source = -k % GROUP
        tile = tiles[source]
        turned.append(pltpu.roll(tile, BRICK * source, axis) if source else tile)
    step = 1
    while step < GROUP:
        moved = (block // step) % 2 == 1
        turned = [
            jnp.where(moved, turned[(k - step) % GROUP], turned[k]) for k in range(GROUP)
        ]
        step *= 2
    return [
        pltpu.roll(turned[k], LANES - BRICK * k, axis) if k else turned[k] for k in range(GROUP)
    ]


def fill_slots(me_ref, owners_ref, slots_ref, counts_ref, capacity):
    def clear(member, carry):
        counts_ref[member] = 0
        return carry

    lax.fori_loop(0, counts_ref.shape[0], clear, 0)

    def place(brick, carry):
        owner = owners_ref[brick]
        rank = counts_ref[owner]
        slots_ref[brick] = (owner ^ me_ref[0]) * capacity + rank
        counts_ref[owner] = rank + 1
        return carry

    lax.fori_loop(0, slots_ref.shape[0], place, 0)


def copy_all(pairs, sems):
    copies = [
        pltpu.make_async_copy(source, target, sems.at[i])
        for i, (source, target) in enumerate(pairs)
    ]
    for copy in copies:
        copy.start()
    return copies


def columns_of(ref, row, across):
    return jnp.concatenate(
        [ref[row + dx, across + dy] for dx in range(3) for dy in range(3)], axis=0
    )


def conv_two(kernel, ref, row, across):
    channels = ref.shape[2]
    stacked = jnp.concatenate(
        [columns_of(ref, row, across), columns_of(ref, row, across + 1)], axis=1
    )
    product = jnp.dot(kernel, stacked, preferred_element_type=jnp.float32)
    results = []
    for half in range(2):
        part = product[:, half * LANES : (half + 1) * LANES]
        results.append(
            shift_lanes(part[:channels], 1)
            + part[channels : 2 * channels]
            + shift_lanes(part[2 * channels :], -1)
        )
    return results


def fill_padded(padded_ref, y_low, y_high, x_low, x_high):
    rows, across = padded_ref.shape[0] - 2, padded_ref.shape[1] - 2
    for y in range(across + 2):
        padded_ref[0, y] = x_low[0, y]
        padded_ref[rows + 1, y] = x_high[0, y]
    for x in range(rows):
        padded_ref[x + 1, 0] = y_low[x, 0]
        padded_ref[x + 1, across + 1] = y_high[x, 0]


def forward_body(
    members,
    me_ref,
    owners_ref,
    features_ref,
    mask_ref,
    y_low,
    y_high,
    x_low,
    x_high,
    weight_ref,
    bias_ref,
    *refs,
):
    messages, refs = refs[:members], refs[members:]
    padded_ref, factor_ref, backward_ref = refs[:3]
    outgoing_ref, scene_ref, kernel_ref, slots_ref, counts_ref, sems = refs[3:]
    rows, across, channels, _ = features_ref.shape
    capacity = messages[0].shape[0]
    fill_slots(me_ref, owners_ref, slots_ref, counts_ref, capacity)
    fill_padded(padded_ref, y_low, y_high, x_low, x_high)
    for shift in range(3):
        mirrored = slice((2 - shift) * channels, (3 - shift) * channels)
        taken = slice(shift * channels, (shift + 1) * channels)
        for tap in range(9):
            placed = slice(tap * channels, (tap + 1) * channels)
            kernel_ref[taken, placed] = weight_ref[tap, :, taken]
            backward_ref[taken, placed] = weight_ref[8 - tap, :, mirrored].T

    @pl.loop(0, rows)
    def _(x):
        for y in range(across):
            half = mask_ref[x, y : y + 1, :].astype(jnp.float32)
            padded_ref[x + 1, y + 1] = (
                features_ref[x, y].astype(jnp.float32) * half
            ).astype(jnp.bfloat16)

    @pl.loop(0, outgoing_ref.shape[0])
    def _(slot):
        outgoing_ref[slot] = jnp.zeros(outgoing_ref.shape[1:], outgoing_ref.dtype)

    bias = bias_ref[...]

    @pl.loop(0, rows)
    def _(x):
        for y in range(0, across, 2):
            for half, summed in enumerate(conv_two(kernel_ref[...], padded_ref, x, y)):
                preact = summed + bias
                gating = jax.nn.sigmoid(preact)
                active = mask_ref[x, y + half : y + half + 1, :].astype(jnp.float32)
                gated = active * gating
                scene_ref[x * across + y + half] = (preact * gated).astype(scene_ref.dtype)
                factor_ref[x, y + half] = gated * (1.0 + preact * (1.0 - gating))

    for group in range(rows * across // GROUP):

        @pl.loop(0, channels // CHUNK)
        def _(part):
            span = pl.ds(pl.multiple_of(part * CHUNK, CHUNK), CHUNK)
            tiles = swap_blocks([scene_ref[group * GROUP + q, span, :] for q in range(GROUP)])
            for brick in range(GROUP):
                outgoing_ref[
                    slots_ref[brick], span, group * LANES : (group + 1) * LANES
                ] = tiles[brick]

    for copy in copy_all(
        [
            (outgoing_ref.at[k * capacity : (k + 1) * capacity], messages[k])
            for k in range(members)
        ],
        sems,
    ):
        copy.wait()


def slope_body(
    capacity, zero_ref, owners_ref, returned_ref, factor_ref, slope_ref, slots_ref, counts_ref
):
    rows, across, channels, _ = factor_ref.shape
    fill_slots(zero_ref, owners_ref, slots_ref, counts_ref, capacity)
    for group in range(rows * across // GROUP):

        @pl.loop(0, channels // CHUNK)
        def _(part):
            span = pl.ds(pl.multiple_of(part * CHUNK, CHUNK), CHUNK)
            tiles = swap_blocks(
                [
                    returned_ref[
                        slots_ref[brick], span, group * LANES : (group + 1) * LANES
                    ]
                    for brick in range(GROUP)
                ]
            )
            for q in range(GROUP):
                x, y = (group * GROUP + q) // across, (group * GROUP + q) % across
                slope_ref[x, y, span, :] = (
                    tiles[q].astype(jnp.float32) * factor_ref[x, y, span, :]
                ).astype(slope_ref.dtype)


def kernel_grad_body(slope_ref, padded_ref, parts_ref, total_ref):
    rows, across, channels, _ = slope_ref.shape
    total_ref[...] = jnp.zeros_like(total_ref)

    @pl.loop(0, rows)
    def _(x):
        for y in range(0, across, 2):
            shifted = []
            for half in range(2):
                block = slope_ref[x, y + half].astype(jnp.float32)
                shifted.append(
                    jnp.concatenate(
                        [shift_lanes(block, -1), block, shift_lanes(block, 1)], axis=0
                    ).astype(jnp.bfloat16)
                )
            left = jnp.concatenate(shifted, axis=1)
            right = jnp.concatenate(
                [columns_of(padded_ref, x, y), columns_of(padded_ref, x, y + 1)], axis=1
            )
            total_ref[...] += lax.dot_general(
                left, right, (((1,), (1,)), ((), ())), preferred_element_type=jnp.float32
            )

    split, _, share, _ = parts_ref.shape
    for part in range(split):
        for shift in range(3):
            start = shift * channels + part * share
            parts_ref[part, shift] = total_ref[start : start + share, :]


def finish_body(scale, at_ref, *refs):
    pieces, out_ref, shares_ref = refs[:-2], refs[-2], refs[-1]
    split, _, share, _ = shares_ref.shape
    for index, piece in enumerate(pieces):
        shares_ref[at_ref[index]] = piece[...].astype(jnp.float32) * scale
    channels = split * share
    for part in range(split):
        for shift in range(3):
            for tap in range(9):
                out_ref[
                    tap,
                    part * share : (part + 1) * share,
                    shift * channels : (shift + 1) * channels,
                ] = shares_ref[part, shift, :, tap * channels : (tap + 1) * channels]


def features_grad_body(
    slope_ref,
    mask_ref,
    y_low,
    y_high,
    x_low,
    x_high,
    kernel_ref,
    out_ref,
    padded_ref,
):
    rows, across, channels, _ = slope_ref.shape
    fill_padded(padded_ref, y_low, y_high, x_low, x_high)

    @pl.loop(0, rows)
    def _(x):
        for y in range(across):
            padded_ref[x + 1, y + 1] = slope_ref[x, y]

    @pl.loop(0, rows)
    def _(x):
        for y in range(0, across, 2):
            for half, summed in enumerate(conv_two(kernel_ref[...], padded_ref, x, y)):
                active = mask_ref[x, y + half : y + half + 1, :].astype(jnp.float32)
                out_ref[x, y + half] = (active * summed).astype(out_ref.dtype)


def call(body, outs, specs, out_specs, scratch, args, flops, bytes_accessed, transcendentals=0):
    return pl.pallas_call(
        body,
        out_shape=outs,
        in_specs=specs,
        out_specs=out_specs,
        scratch_shapes=scratch,
        compiler_params=pltpu.CompilerParams(vmem_limit_bytes=VMEM_LIMIT),
        cost_estimate=pl.CostEstimate(
            flops=flops, bytes_accessed=bytes_accessed, transcendentals=transcendentals
        ),
    )(*args)


def after(values, *others):
    return lax.optimization_barrier((tuple(values), others))[0]


def from_neighbours(low_edge, high_edge, axis):
    count = lax.axis_size(axis)
    forward = [(i, i + 1) for i in range(count - 1)]
    backward = [(target, source) for source, target in forward]
    return lax.ppermute(high_edge, axis, forward), lax.ppermute(low_edge, axis, backward)


def halo_rows(rows, y_low, y_high):
    pieces = (slice(0, 1), slice(-1, None))
    return from_neighbours(
        *[
            jnp.concatenate([y_low[piece], row, y_high[piece]], axis=1)
            for row, piece in zip(rows, pieces)
        ],
        "gx",
    )


def edge_of(array):
    def edge(side, along_x):
        piece = slice(0, 1) if side == 0 else slice(-1, None)
        return array[piece] if along_x else array[:, piece]

    return edge


def from_group(value, axis, radix, stride):
    count = lax.axis_size(axis)
    return [
        lax.ppermute(value, axis, [(i, i ^ (k * stride)) for i in range(count)])
        for k in range(1, radix)
    ]


def to_members(blocks, differences):
    count = lax.axis_size("gy")
    return {
        k: lax.ppermute(blocks[k], "gy", [(i, i ^ k) for i in range(count)]) for k in differences
    }


def on_device(features, active_mask, owners, weight, channel_bias, cotangent):
    rows, across, channels, column = features.shape
    members_x, members = lax.axis_size("gx"), lax.axis_size("gy")
    at_x, me = lax.axis_index("gx"), lax.axis_index("gy")
    capacity = cotangent.shape[1] // members
    slot_count = members * capacity
    brick = cotangent.shape[3]
    vmem = pl.BlockSpec(memory_space=pltpu.VMEM)
    smem = pl.BlockSpec(memory_space=pltpu.SMEM)
    anywhere = pl.BlockSpec(memory_space=pltpu.HBM)
    conv_flops = 2 * rows * across * column * 27 * channels * channels
    scene_bytes = rows * across * column * channels
    far = [list(range(members // 2, members))[i::4] for i in range(4)]
    near = list(range(1, members // 2))
    message = (capacity, channels, brick)
    packed = jax.ShapeDtypeStruct(message, jnp.bfloat16)

    def masked(scene):
        def edge(side, along_x):
            mask = edge_of(active_mask)(side, along_x).astype(jnp.bfloat16)
            return edge_of(scene)(side, along_x) * mask[:, :, None, :]

        return edge

    columns = [masked(features)(side, False) for side in (0, -1)]
    halo = from_neighbours(*columns, "gy")
    rows_beside = [masked(features)(side, True) for side in (0, -1)]
    (owned,) = after([cotangent], *halo)
    returned = lax.all_to_all(
        owned.reshape(members, capacity * channels, brick),
        "gy",
        split_axis=0,
        concat_axis=0,
        tiled=True,
    ).reshape(slot_count, channels, brick)
    halo = (*halo, *halo_rows(rows_beside, *halo))

    me_list = me.reshape(1).astype(jnp.int32)
    owner_list = owners.reshape(-1)
    table = [pltpu.SMEM((owner_list.size,), jnp.int32), pltpu.SMEM((members,), jnp.int32)]
    slots = pltpu.VMEM((slot_count, channels, brick), jnp.bfloat16)
    sems = pltpu.SemaphoreType.DMA((members,))
    padded_shape = (rows + 2, across + 2, channels, column)
    kernel_shape = (3 * channels, 9 * channels)
    *outgoing, padded, factor, backward_kernel = call(
        functools.partial(forward_body, members),
        (
            *[packed] * members,
            jax.ShapeDtypeStruct(padded_shape, jnp.bfloat16),
            jax.ShapeDtypeStruct(features.shape, jnp.float32),
            jax.ShapeDtypeStruct(kernel_shape, jnp.bfloat16),
        ),
        [smem] * 2 + [vmem] * 8,
        [anywhere] * members + [vmem] * 3,
        [
            slots,
            pltpu.VMEM((rows * across, channels, column), jnp.bfloat16),
            pltpu.VMEM(kernel_shape, jnp.bfloat16),
            *table,
            sems,
        ],
        (
            me_list,
            owner_list,
            features,
            active_mask,
            *halo,
            weight.reshape(9, channels, 3 * channels),
            channel_bias.reshape(channels, 1),
        ),
        conv_flops,
        14 * scene_bytes,
        2 * scene_bytes,
    )
    arrived = {0: outgoing[0]}

    def send(differences, *others):
        messages = after([outgoing[k] for k in differences], *others)
        arrived.update(to_members(dict(zip(differences, messages)), differences))

    arrived.update(to_members(outgoing, near))
    (returned,) = after([returned], *[arrived[k] for k in near])
    slope = call(
        functools.partial(slope_body, capacity),
        jax.ShapeDtypeStruct(features.shape, jnp.bfloat16),
        [smem] * 2 + [vmem] * 2,
        vmem,
        [*table],
        (jnp.zeros((1,), jnp.int32), owner_list, returned, factor),
        0,
        0,
    )

    def in_turn(value, index):
        return after([value], *[arrived[k] for k in far[index]])[0]

    send(far[0], returned)
    send(far[1], returned)
    shares = call(
        kernel_grad_body,
        jax.ShapeDtypeStruct((members_x, 3, channels // members_x, 9 * channels), jnp.float32),
        [vmem] * 2,
        vmem,
        [pltpu.VMEM(kernel_shape, jnp.float32)],
        (slope, padded),
        0,
        0,
    )
    send(far[2], shares)
    shares = in_turn(shares, 0)
    total = lax.dynamic_index_in_dim(shares, at_x, 0, keepdims=False)
    for k in range(1, members_x):
        wanted = lax.dynamic_index_in_dim(shares, at_x ^ k, 0, keepdims=False)
        total = total + lax.ppermute(
            wanted.astype(jnp.bfloat16), "gx", [(i, i ^ k) for i in range(members_x)]
        ).astype(jnp.float32)
    columns = [edge_of(slope)(side, False) for side in (0, -1)]
    slope_halo = from_neighbours(*after(columns, total), "gy")
    send(far[3], total)
    for index, (radix, stride) in enumerate(((members // 4, 1), (4, members // 4))):
        total = in_turn(total, index + 1)
        sent = total.astype(jnp.bfloat16)
        terms = [
            term.astype(jnp.float32) for term in [sent, *from_group(sent, "gy", radix, stride)]
        ]
        while len(terms) > 1:
            terms = [terms[i] + terms[i + 1] for i in range(0, len(terms), 2)]
        total = terms[0]
    mine = total.astype(jnp.bfloat16)
    at_shares = jnp.stack([at_x ^ k for k in range(members_x)]).astype(jnp.int32)
    pieces = [mine, *from_group(mine, "gx", members_x, 1)]
    pieces = after(pieces, *[arrived[k] for k in far[3]])
    voxel_total = rows * across * column * members_x * members
    grad_weight = call(
        functools.partial(finish_body, voxel_total ** (-0.5)),
        jax.ShapeDtypeStruct((9, channels, 3 * channels), jnp.float32),
        [smem] + [vmem] * members_x,
        vmem,
        [pltpu.VMEM(shares.shape, jnp.float32)],
        (at_shares, *pieces),
        weight.size,
        6 * weight.size,
    ).reshape(weight.shape)
    rows_beside = [edge_of(slope)(side, True) for side in (0, -1)]
    slope_halo = (*slope_halo, *halo_rows(rows_beside, *slope_halo))
    grad_features = call(
        features_grad_body,
        jax.ShapeDtypeStruct(features.shape, jnp.bfloat16),
        [vmem] * 7,
        vmem,
        [pltpu.VMEM(padded_shape, jnp.bfloat16)],
        (slope, active_mask, *slope_halo, backward_kernel),
        0,
        0,
    )
    activations = jnp.zeros((members, *message), jnp.bfloat16)
    for k in [0, *near, *far[0], *far[1], *far[2], *far[3]]:
        activations = lax.dynamic_update_index_in_dim(activations, arrived[k], me ^ k, 0)
    activations = activations.reshape(1, slot_count, channels, brick)
    return activations, grad_features, grad_weight


def solution(mesh):
    in_specs = (
        P("gx", "gy", None, None),
        P("gx", "gy", None),
        P("gx", "gy", None),
        P(),
        P(),
        P("gx", "gy", None, None),
    )
    out_specs = (P("gx", "gy", None, None), P("gx", "gy", None, None), P())
    return jax.shard_map(
        on_device, mesh=mesh, in_specs=in_specs, out_specs=out_specs, check_vma=False
    )
```

```python
import functools

import jax
import jax.numpy as jnp
from jax import lax
from jax.experimental import pallas as pl
from jax.experimental.pallas import tpu as pltpu
from jax.sharding import PartitionSpec as P

BRICK = 8
LANES = 128
GROUP = LANES // BRICK
CHUNK = 32
VMEM_LIMIT = 48 * 2**20


def shift_lanes(value, by):
    width = value.shape[-1]
    lane = lax.broadcasted_iota(jnp.int32, value.shape, value.ndim - 1)
    rolled = pltpu.roll(value, by % width, value.ndim - 1)
    inside = lane >= by if by > 0 else lane < width + by
    return jnp.where(inside, rolled, jnp.zeros_like(rolled))


def swap_blocks(tiles):
    axis = tiles[0].ndim - 1
    block = lax.broadcasted_iota(jnp.int32, tiles[0].shape, axis) // BRICK
    turned = []
    for k in range(GROUP):
        source = -k % GROUP
        tile = tiles[source]
        turned.append(pltpu.roll(tile, BRICK * source, axis) if source else tile)
    step = 1
    while step < GROUP:
        moved = (block // step) % 2 == 1
        turned = [
            jnp.where(moved, turned[(k - step) % GROUP], turned[k]) for k in range(GROUP)
        ]
        step *= 2
    return [
        pltpu.roll(turned[k], LANES - BRICK * k, axis) if k else turned[k] for k in range(GROUP)
    ]


def fill_slots(me_ref, owners_ref, slots_ref, counts_ref, capacity):
    def clear(member, carry):
        counts_ref[member] = 0
        return carry

    lax.fori_loop(0, counts_ref.shape[0], clear, 0)

    def place(brick, carry):
        owner = owners_ref[brick]
        rank = counts_ref[owner]
        slots_ref[brick] = (owner ^ me_ref[0]) * capacity + rank
        counts_ref[owner] = rank + 1
        return carry

    lax.fori_loop(0, slots_ref.shape[0], place, 0)


def copy_all(pairs, sems):
    copies = [
        pltpu.make_async_copy(source, target, sems.at[i])
        for i, (source, target) in enumerate(pairs)
    ]
    for copy in copies:
        copy.start()
    return copies


def columns_of(ref, row, across):
    return jnp.concatenate(
        [ref[row + dx, across + dy] for dx in range(3) for dy in range(3)], axis=0
    )


def conv_two(kernel, ref, row, across):
    channels = ref.shape[2]
    stacked = jnp.concatenate(
        [columns_of(ref, row, across), columns_of(ref, row, across + 1)], axis=1
    )
    product = jnp.dot(kernel, stacked, preferred_element_type=jnp.float32)
    results = []
    for half in range(2):
        part = product[:, half * LANES : (half + 1) * LANES]
        results.append(
            shift_lanes(part[:channels], 1)
            + part[channels : 2 * channels]
            + shift_lanes(part[2 * channels :], -1)
        )
    return results


def fill_padded(padded_ref, y_low, y_high, x_low, x_high):
    rows, across = padded_ref.shape[0] - 2, padded_ref.shape[1] - 2
    for y in range(across + 2):
        padded_ref[0, y] = x_low[0, y]
        padded_ref[rows + 1, y] = x_high[0, y]
    for x in range(rows):
        padded_ref[x + 1, 0] = y_low[x, 0]
        padded_ref[x + 1, across + 1] = y_high[x, 0]


def forward_body(
    members,
    me_ref,
    owners_ref,
    features_ref,
    mask_ref,
    y_low,
    y_high,
    x_low,
    x_high,
    weight_ref,
    bias_ref,
    *refs,
):
    messages, refs = refs[:members], refs[members:]
    padded_ref, factor_ref, backward_ref = refs[:3]
    outgoing_ref, scene_ref, kernel_ref, slots_ref, counts_ref, sems = refs[3:]
    rows, across, channels, _ = features_ref.shape
    capacity = messages[0].shape[0]
    fill_slots(me_ref, owners_ref, slots_ref, counts_ref, capacity)
    fill_padded(padded_ref, y_low, y_high, x_low, x_high)
    for shift in range(3):
        mirrored = slice((2 - shift) * channels, (3 - shift) * channels)
        taken = slice(shift * channels, (shift + 1) * channels)
        for tap in range(9):
            placed = slice(tap * channels, (tap + 1) * channels)
            kernel_ref[taken, placed] = weight_ref[tap, :, taken]
            backward_ref[taken, placed] = weight_ref[8 - tap, :, mirrored].T

    @pl.loop(0, rows)
    def _(x):
        for y in range(across):
            half = mask_ref[x, y : y + 1, :].astype(jnp.float32)
            padded_ref[x + 1, y + 1] = (
                features_ref[x, y].astype(jnp.float32) * half
            ).astype(jnp.bfloat16)

    @pl.loop(0, outgoing_ref.shape[0])
    def _(slot):
        outgoing_ref[slot] = jnp.zeros(outgoing_ref.shape[1:], outgoing_ref.dtype)

    bias = bias_ref[...]

    @pl.loop(0, rows)
    def _(x):
        for y in range(0, across, 2):
            for half, summed in enumerate(conv_two(kernel_ref[...], padded_ref, x, y)):
                preact = summed + bias
                gating = jax.nn.sigmoid(preact)
                active = mask_ref[x, y + half : y + half + 1, :].astype(jnp.float32)
                gated = active * gating
                scene_ref[x * across + y + half] = (preact * gated).astype(scene_ref.dtype)
                factor_ref[x, y + half] = gated * (1.0 + preact * (1.0 - gating))

    for group in range(rows * across // GROUP):

        @pl.loop(0, channels // CHUNK)
        def _(part):
            span = pl.ds(pl.multiple_of(part * CHUNK, CHUNK), CHUNK)
            tiles = swap_blocks([scene_ref[group * GROUP + q, span, :] for q in range(GROUP)])
            for brick in range(GROUP):
                outgoing_ref[
                    slots_ref[brick], span, group * LANES : (group + 1) * LANES
                ] = tiles[brick]

    for copy in copy_all(
        [
            (outgoing_ref.at[k * capacity : (k + 1) * capacity], messages[k])
            for k in range(members)
        ],
        sems,
    ):
        copy.wait()


def slope_body(
    capacity, zero_ref, owners_ref, returned_ref, factor_ref, slope_ref, slots_ref, counts_ref
):
    rows, across, channels, _ = factor_ref.shape
    fill_slots(zero_ref, owners_ref, slots_ref, counts_ref, capacity)
    for group in range(rows * across // GROUP):

        @pl.loop(0, channels // CHUNK)
        def _(part):
            span = pl.ds(pl.multiple_of(part * CHUNK, CHUNK), CHUNK)
            tiles = swap_blocks(
                [
                    returned_ref[
                        slots_ref[brick], span, group * LANES : (group + 1) * LANES
                    ]
                    for brick in range(GROUP)
                ]
            )
            for q in range(GROUP):
                x, y = (group * GROUP + q) // across, (group * GROUP + q) % across
                slope_ref[x, y, span, :] = (
                    tiles[q].astype(jnp.float32) * factor_ref[x, y, span, :]
                ).astype(slope_ref.dtype)


def kernel_grad_body(slope_ref, padded_ref, parts_ref, total_ref):
    rows, across, channels, _ = slope_ref.shape
    total_ref[...] = jnp.zeros_like(total_ref)

    @pl.loop(0, rows)
    def _(x):
        for y in range(0, across, 2):
            shifted = []
            for half in range(2):
                block = slope_ref[x, y + half].astype(jnp.float32)
                shifted.append(
                    jnp.concatenate(
                        [shift_lanes(block, -1), block, shift_lanes(block, 1)], axis=0
                    ).astype(jnp.bfloat16)
                )
            left = jnp.concatenate(shifted, axis=1)
            right = jnp.concatenate(
                [columns_of(padded_ref, x, y), columns_of(padded_ref, x, y + 1)], axis=1
            )
            total_ref[...] += lax.dot_general(
                left, right, (((1,), (1,)), ((), ())), preferred_element_type=jnp.float32
            )

    split, _, share, _ = parts_ref.shape
    for part in range(split):
        for shift in range(3):
            start = shift * channels + part * share
            parts_ref[part, shift] = total_ref[start : start + share, :]


def finish_body(scale, at_ref, *refs):
    pieces, out_ref, shares_ref = refs[:-2], refs[-2], refs[-1]
    split, _, share, _ = shares_ref.shape
    for index, piece in enumerate(pieces):
        shares_ref[at_ref[index]] = piece[...].astype(jnp.float32) * scale
    channels = split * share
    for part in range(split):
        for shift in range(3):
            for tap in range(9):
                out_ref[
                    tap,
                    part * share : (part + 1) * share,
                    shift * channels : (shift + 1) * channels,
                ] = shares_ref[part, shift, :, tap * channels : (tap + 1) * channels]


def features_grad_body(
    slope_ref,
    mask_ref,
    y_low,
    y_high,
    x_low,
    x_high,
    kernel_ref,
    out_ref,
    padded_ref,
):
    rows, across, channels, _ = slope_ref.shape
    fill_padded(padded_ref, y_low, y_high, x_low, x_high)

    @pl.loop(0, rows)
    def _(x):
        for y in range(across):
            padded_ref[x + 1, y + 1] = slope_ref[x, y]

    @pl.loop(0, rows)
    def _(x):
        for y in range(0, across, 2):
            for half, summed in enumerate(conv_two(kernel_ref[...], padded_ref, x, y)):
                active = mask_ref[x, y + half : y + half + 1, :].astype(jnp.float32)
                out_ref[x, y + half] = (active * summed).astype(out_ref.dtype)


def call(body, outs, specs, out_specs, scratch, args, flops, bytes_accessed, transcendentals=0):
    return pl.pallas_call(
        body,
        out_shape=outs,
        in_specs=specs,
        out_specs=out_specs,
        scratch_shapes=scratch,
        compiler_params=pltpu.CompilerParams(vmem_limit_bytes=VMEM_LIMIT),
        cost_estimate=pl.CostEstimate(
            flops=flops, bytes_accessed=bytes_accessed, transcendentals=transcendentals
        ),
    )(*args)


def after(values, *others):
    return lax.optimization_barrier((tuple(values), others))[0]


def from_neighbours(low_edge, high_edge, axis):
    count = lax.axis_size(axis)
    forward = [(i, i + 1) for i in range(count - 1)]
    backward = [(target, source) for source, target in forward]
    return lax.ppermute(high_edge, axis, forward), lax.ppermute(low_edge, axis, backward)


def halo_rows(rows, y_low, y_high):
    pieces = (slice(0, 1), slice(-1, None))
    return from_neighbours(
        *[
            jnp.concatenate([y_low[piece], row, y_high[piece]], axis=1)
            for row, piece in zip(rows, pieces)
        ],
        "gx",
    )


def edge_of(array):
    def edge(side, along_x):
        piece = slice(0, 1) if side == 0 else slice(-1, None)
        return array[piece] if along_x else array[:, piece]

    return edge


def from_group(value, axis, radix, stride):
    count = lax.axis_size(axis)
    return [
        lax.ppermute(value, axis, [(i, i ^ (k * stride)) for i in range(count)])
        for k in range(1, radix)
    ]


def to_members(blocks, differences):
    count = lax.axis_size("gy")
    return {
        k: lax.ppermute(blocks[k], "gy", [(i, i ^ k) for i in range(count)]) for k in differences
    }


def on_device(features, active_mask, owners, weight, channel_bias, cotangent):
    rows, across, channels, column = features.shape
    members_x, members = lax.axis_size("gx"), lax.axis_size("gy")
    at_x, me = lax.axis_index("gx"), lax.axis_index("gy")
    capacity = cotangent.shape[1] // members
    slot_count = members * capacity
    brick = cotangent.shape[3]
    vmem = pl.BlockSpec(memory_space=pltpu.VMEM)
    smem = pl.BlockSpec(memory_space=pltpu.SMEM)
    anywhere = pl.BlockSpec(memory_space=pltpu.HBM)
    conv_flops = 2 * rows * across * column * 27 * channels * channels
    scene_bytes = rows * across * column * channels
    far = [list(range(members // 2, members))[i::4] for i in range(4)]
    near = list(range(1, members // 2))
    message = (capacity, channels, brick)
    packed = jax.ShapeDtypeStruct(message, jnp.bfloat16)

    def masked(scene):
        def edge(side, along_x):
            mask = edge_of(active_mask)(side, along_x).astype(jnp.bfloat16)
            return edge_of(scene)(side, along_x) * mask[:, :, None, :]

        return edge

    columns = [masked(features)(side, False) for side in (0, -1)]
    halo = from_neighbours(*columns, "gy")
    rows_beside = [masked(features)(side, True) for side in (0, -1)]
    (owned,) = after([cotangent], *halo)
    returned = lax.all_to_all(
        owned.reshape(members, capacity * channels, brick),
        "gy",
        split_axis=0,
        concat_axis=0,
        tiled=True,
    ).reshape(slot_count, channels, brick)
    halo = (*halo, *halo_rows(rows_beside, *halo))

    me_list = me.reshape(1).astype(jnp.int32)
    owner_list = owners.reshape(-1)
    table = [pltpu.SMEM((owner_list.size,), jnp.int32), pltpu.SMEM((members,), jnp.int32)]
    slots = pltpu.VMEM((slot_count, channels, brick), jnp.bfloat16)
    sems = pltpu.SemaphoreType.DMA((members,))
    padded_shape = (rows + 2, across + 2, channels, column)
    kernel_shape = (3 * channels, 9 * channels)
    *outgoing, padded, factor, backward_kernel = call(
        functools.partial(forward_body, members),
        (
            *[packed] * members,
            jax.ShapeDtypeStruct(padded_shape, jnp.bfloat16),
            jax.ShapeDtypeStruct(features.shape, jnp.float32),
            jax.ShapeDtypeStruct(kernel_shape, jnp.bfloat16),
        ),
        [smem] * 2 + [vmem] * 8,
        [anywhere] * members + [vmem] * 3,
        [
            slots,
            pltpu.VMEM((rows * across, channels, column), jnp.bfloat16),
            pltpu.VMEM(kernel_shape, jnp.bfloat16),
            *table,
            sems,
        ],
        (
            me_list,
            owner_list,
            features,
            active_mask,
            *halo,
            weight.reshape(9, channels, 3 * channels),
            channel_bias.reshape(channels, 1),
        ),
        conv_flops,
        14 * scene_bytes,
        2 * scene_bytes,
    )
    arrived = {0: outgoing[0]}

    def send(differences, *others):
        messages = after([outgoing[k] for k in differences], *others)
        arrived.update(to_members(dict(zip(differences, messages)), differences))

    arrived.update(to_members(outgoing, near))
    (returned,) = after([returned], *[arrived[k] for k in near])
    slope = call(
        functools.partial(slope_body, capacity),
        jax.ShapeDtypeStruct(features.shape, jnp.bfloat16),
        [smem] * 2 + [vmem] * 2,
        vmem,
        [*table],
        (jnp.zeros((1,), jnp.int32), owner_list, returned, factor),
        0,
        0,
    )

    def in_turn(value, index):
        return after([value], *[arrived[k] for k in far[index]])[0]

    send(far[0], returned)
    send(far[1], returned)
    shares = call(
        kernel_grad_body,
        jax.ShapeDtypeStruct((members_x, 3, channels // members_x, 9 * channels), jnp.float32),
        [vmem] * 2,
        vmem,
        [pltpu.VMEM(kernel_shape, jnp.float32)],
        (slope, padded),
        0,
        0,
    )
    send(far[2], shares)
    shares = in_turn(shares, 0)
    total = lax.dynamic_index_in_dim(shares, at_x, 0, keepdims=False)
    for k in range(1, members_x):
        wanted = lax.dynamic_index_in_dim(shares, at_x ^ k, 0, keepdims=False)
        total = total + lax.ppermute(
            wanted.astype(jnp.bfloat16), "gx", [(i, i ^ k) for i in range(members_x)]
        ).astype(jnp.float32)
    columns = [edge_of(slope)(side, False) for side in (0, -1)]
    slope_halo = from_neighbours(*after(columns, shares), "gy")
    for index, (radix, stride) in enumerate(((members // 4, 1), (4, members // 4))):
        total = in_turn(total, index + 1)
        sent = total.astype(jnp.bfloat16)
        terms = [
            term.astype(jnp.float32) for term in [sent, *from_group(sent, "gy", radix, stride)]
        ]
        while len(terms) > 1:
            terms = [terms[i] + terms[i + 1] for i in range(0, len(terms), 2)]
        total = terms[0]
        if index == 0:
            send(far[3], total)
    mine = total.astype(jnp.bfloat16)
    at_shares = jnp.stack([at_x ^ k for k in range(members_x)]).astype(jnp.int32)
    pieces = [mine, *from_group(mine, "gx", members_x, 1)]
    pieces = after(pieces, *[arrived[k] for k in far[3]])
    voxel_total = rows * across * column * members_x * members
    grad_weight = call(
        functools.partial(finish_body, voxel_total ** (-0.5)),
        jax.ShapeDtypeStruct((9, channels, 3 * channels), jnp.float32),
        [smem] + [vmem] * members_x,
        vmem,
        [pltpu.VMEM(shares.shape, jnp.float32)],
        (at_shares, *pieces),
        weight.size,
        6 * weight.size,
    ).reshape(weight.shape)
    rows_beside = [edge_of(slope)(side, True) for side in (0, -1)]
    slope_halo = (*slope_halo, *halo_rows(rows_beside, *slope_halo))
    grad_features = call(
        features_grad_body,
        jax.ShapeDtypeStruct(features.shape, jnp.bfloat16),
        [vmem] * 7,
        vmem,
        [pltpu.VMEM(padded_shape, jnp.bfloat16)],
        (slope, active_mask, *slope_halo, backward_kernel),
        conv_flops,
        5 * scene_bytes,
    )
    activations = jnp.zeros((members, *message), jnp.bfloat16)
    for k in [0, *near, *far[0], *far[1], *far[2], *far[3]]:
        activations = lax.dynamic_update_index_in_dim(activations, arrived[k], me ^ k, 0)
    activations = activations.reshape(1, slot_count, channels, brick)
    return activations, grad_features, grad_weight


def solution(mesh):
    in_specs = (
        P("gx", "gy", None, None),
        P("gx", "gy", None),
        P("gx", "gy", None),
        P(),
        P(),
        P("gx", "gy", None, None),
    )
    out_specs = (P("gx", "gy", None, None), P("gx", "gy", None, None), P())
    return jax.shard_map(
        on_device, mesh=mesh, in_specs=in_specs, out_specs=out_specs, check_vma=False
    )
```
